512 devices in a mesh: expert: 64 (over z, y), dp: 8 (over x, core).
Axes of the slice: x: 4, y: 8, z: 8, core: 2. Of those that a mesh axis runs over, the one named last changes fastest.
Arguments:
- tokens: bfloat16 [8192, 4096], P('expert', 'dp'), may hold values from -6 to 6
- route_ids: int32 [8192, 8], P('expert'), may hold values from 0 to 63, as said below
- route_gates: float32 [8192, 8], P('expert'), may hold values from 0.05 to 0.5
- keep_mask: int32 [8192, 8], P('expert'), may hold values from 0 to 1, as said below
- old_gate: bfloat16 [64, 4096, 768], P('expert', 'dp'), may hold values from -0.09375 to 0.09375
- old_up: bfloat16 [64, 4096, 768], P('expert', 'dp'), may hold values from -0.09375 to 0.09375
- old_down: bfloat16 [64, 768, 4096], P('expert', None, 'dp'), may hold values from -0.21875 to 0.21875
- placement_map: int32 [64], replicated, may hold values from 0 to 63, each once
Outputs:
- mixed: bfloat16 [8192, 4096], P('expert', 'dp')
- new_gate: bfloat16 [64, 4096, 768], P('expert', 'dp')
- new_up: bfloat16 [64, 4096, 768], P('expert', 'dp')
- new_down: bfloat16 [64, 768, 4096], P('expert', None, 'dp')
The draws below stay inside these ranges and needn't reach their ends.
Inputs may be any that keep to these rules, and one draw needn't show every extreme that they name: `route_ids`: each token's 8 slots are distinct. `keep_mask`: in each token group of 128 tokens at most 16 kept assignments name any one slot, and in every group some slot has exactly 16; dropped assignments are those past the first 16 of their slot in the group's order of tokens and k.
All inputs are finite; a program needn't handle non-finite values.
Results may differ from the reference program's by a relative error of at most 0.015.
Values may be sent and summed in bfloat16 or wider, within the bound.
No kernel may reach another device: no remote copies, remote signals or barrier semaphores. Data moves between devices by JAX's collectives and lax.ppermute only.
A program may use at most 64 MiB of HBM per device.

```python
import math
import jax
import jax.numpy as jnp
from jax import lax

D = 4096
HIDDEN_SIZE = 768
TOPK = 8
REPLICAS = 64
TOK_GRP = 128
CAP = 16
TOKENS = 8192
N_DP = 8


def routing_helper(key):
    key_base, key_levels, key_hottest = jax.random.split(key, 3)
    columns = jnp.arange(REPLICAS, dtype=jnp.int32)
    scores = jax.random.randint(key_base, (TOKENS, REPLICAS), 0, 4096) * REPLICAS + columns[None, :]
    levels = jax.random.randint(key_levels, (REPLICAS,), 0, 4)
    hottest = jax.random.randint(key_hottest, (), 0, REPLICAS)
    levels = jnp.where(columns == hottest, 8, levels)
    scores = scores + levels[None, :] * (1024 * REPLICAS)
    ignored, chosen = lax.top_k(scores, TOPK)
    chosen = chosen.astype(jnp.int32)
    grouped = chosen.reshape(TOKENS // TOK_GRP, TOK_GRP * TOPK)
    onehot = (grouped[:, :, None] == columns[None, None, :]).astype(jnp.int32)
    before = jnp.cumsum(onehot, axis=1) - onehot
    ranking = jnp.sum(before * onehot, axis=2)
    kept_flag = (ranking < CAP).astype(jnp.int32).reshape(TOKENS, TOPK)
    return (chosen, kept_flag)


def draw_route_ids(key, part):
    chosen, kept_flag = routing_helper(key)
    return chosen


def draw_keep_mask(key, part):
    chosen, kept_flag = routing_helper(key)
    return kept_flag


def steps_of(stream_key, dims, cuts, low, largest):
    loudness, own = 1.0, jax.random.fold_in(stream_key, 6)
    for dim, parts in cuts:
        steps = jnp.exp(jax.random.uniform(jax.random.fold_in(own, dim), (parts,), jnp.float32, low / len(cuts), largest / len(cuts)))
        loudness = loudness * jnp.repeat(steps, dims[dim] // parts).reshape([-1 if axis == dim else 1 for axis in range(len(dims))])
    return loudness


def gaussian(own_key, dims, scale, most, shards=(), kind=jnp.bfloat16):
    loudness = steps_of(own_key, dims, shards, -0.22, 0.18) if shards else 1.0
    values = jax.random.normal(own_key, dims, jnp.float32) * scale * loudness
    return jnp.minimum(jnp.maximum(values, -most), most).astype(kind)


def setup_inputs(seed: int = 0) -> dict:
    arg_keys = jax.random.split(jax.random.key(seed), 9)
    return {
        "tokens": gaussian(arg_keys[0], (TOKENS, D), 1.0, 6.0, ((0, 64), (1, 8))),
        "route_ids": draw_route_ids(jax.random.fold_in(arg_keys[8], 71), 0),
        "route_gates": jnp.clip(jnp.exp(math.log(0.5) - 2.3025851 * jax.random.uniform(arg_keys[2], (TOKENS, TOPK), jnp.float32) ** steps_of(arg_keys[2], (TOKENS, TOPK), ((0, 64),), -0.2, 0.2)), 0.05, 0.5),
        "keep_mask": draw_keep_mask(jax.random.fold_in(arg_keys[8], 71), 0),
        "old_gate": gaussian(arg_keys[4], (REPLICAS, D, HIDDEN_SIZE), D ** -0.5, 0.09375, ((0, 64), (1, 8))),
        "old_up": gaussian(arg_keys[5], (REPLICAS, D, HIDDEN_SIZE), D ** -0.5, 0.09375, ((0, 64), (1, 8))),
        "old_down": gaussian(arg_keys[6], (REPLICAS, HIDDEN_SIZE, D), HIDDEN_SIZE ** -0.5, 0.21875, ((0, 64), (2, 8))),
        "placement_map": jax.random.permutation(arg_keys[7], REPLICAS).astype(jnp.int32),
    }


def reference(tokens, route_ids, route_gates, keep_mask, old_gate, old_up, old_down, placement_map):
    blocks = TOKENS // TOK_GRP
    slot_total = REPLICAS * CAP
    source_of = jnp.zeros((REPLICAS,), jnp.int32).at[placement_map].set(jnp.arange(REPLICAS, dtype=jnp.int32))
    flat_ids = route_ids.reshape(blocks, TOK_GRP * TOPK)
    flat_kept = keep_mask.reshape(blocks, TOK_GRP * TOPK)
    onehot = (flat_ids[:, :, None] == jnp.arange(REPLICAS, dtype=jnp.int32)[None, None, :]).astype(jnp.int32) * flat_kept[:, :, None]
    before = jnp.cumsum(onehot, axis=1) - onehot
    ranking = jnp.sum(before * onehot, axis=2)
    slot_index = jnp.where(flat_kept > 0, flat_ids * CAP + ranking, slot_total)
    token_local = jnp.arange(TOK_GRP * TOPK, dtype=jnp.int32) // TOPK
    token_global = jnp.arange(blocks, dtype=jnp.int32)[:, None] * TOK_GRP + token_local[None, :]
    block_rows = jnp.arange(blocks, dtype=jnp.int32)[:, None]
    table_token = jnp.zeros((blocks, slot_total + 1), jnp.int32).at[block_rows, slot_index].set(token_global)
    table_gate = jnp.zeros((blocks, slot_total + 1), jnp.float32).at[block_rows, slot_index].set(route_gates.reshape(blocks, TOK_GRP * TOPK))
    table_token = table_token[:, :slot_total].reshape(blocks, REPLICAS, CAP)
    table_gate = table_gate[:, :slot_total].reshape(blocks, REPLICAS, CAP)
    width_share = D // N_DP

    def block_sum(split_rows, weight):
        blocked = weight.reshape(N_DP, width_share, HIDDEN_SIZE).astype(jnp.float32)
        partial_value = jnp.einsum("rjd,jdh->jrh", split_rows, blocked, precision=lax.Precision.HIGHEST)
        rounded = lax.optimization_barrier(partial_value.astype(jnp.bfloat16))
        return jnp.sum(rounded.astype(jnp.float32), axis=0)

    def one_replica(totals, replica):
        rows_idx = table_token[:, replica, :].reshape(-1)
        weights_row = table_gate[:, replica, :].reshape(-1)
        anchor = source_of[replica]
        gathered = tokens[rows_idx]
        split_rows = gathered.reshape(-1, N_DP, width_share).astype(jnp.float32)
        gate_sum = block_sum(split_rows, old_gate[anchor])
        up_sum = block_sum(split_rows, old_up[anchor])
        hidden = (jax.nn.silu(gate_sum) * up_sum).astype(jnp.bfloat16)
        expert_out = jnp.dot(hidden, old_down[anchor], preferred_element_type=jnp.float32).astype(jnp.bfloat16)
        weighted = expert_out.astype(jnp.float32) * weights_row[:, None]
        return totals.at[rows_idx].add(weighted), None

    totals, ignored = lax.scan(one_replica, jnp.zeros((TOKENS, D), jnp.float32), jnp.arange(REPLICAS, dtype=jnp.int32))
    mixed = (tokens.astype(jnp.float32) + totals).astype(jnp.bfloat16)
    return (mixed, old_gate[source_of], old_up[source_of], old_down[source_of])
```

```python
import jax
import jax.numpy as jnp
from jax import lax
from jax.experimental import pallas as pl
from jax.experimental.pallas import tpu as pltpu
from jax.sharding import PartitionSpec as P

CAP = 16
LANES = 128
VMEM = pl.BlockSpec(memory_space=pltpu.VMEM)
SMEM = pl.BlockSpec(memory_space=pltpu.SMEM)
F32, BF16, I32 = jnp.float32, jnp.bfloat16, jnp.int32


def call(kernel, out_shape, in_specs, flops=0, moved=0):
    many = isinstance(out_shape, (tuple, list))
    return pl.pallas_call(
        kernel,
        out_shape=out_shape,
        in_specs=in_specs,
        out_specs=[VMEM] * len(out_shape) if many else VMEM,
        compiler_params=pltpu.CompilerParams(vmem_limit_bytes=60 * 1024 * 1024),
        cost_estimate=pl.CostEstimate(flops=flops, bytes_accessed=moved, transcendentals=0),
    )


def dispatch_kernel(ids_ref, keep_ref, map_ref, tokens_ref, out_ref):
    replicas = map_ref.shape[1]
    group = tokens_ref.shape[0]
    ids = jnp.where(keep_ref[...] > 0, ids_ref[...], -1)
    same = lax.broadcasted_iota(I32, (replicas, replicas), 0) == lax.broadcasted_iota(
        I32, (replicas, replicas), 1
    )
    slot_of = jnp.sum(jnp.where(same, map_ref[...], 0), axis=1, keepdims=True)
    wanted = ids[0:1, :] == slot_of
    for k in range(1, ids.shape[0]):
        wanted = wanted | (ids[k : k + 1, :] == slot_of)
    earlier = lax.broadcasted_iota(I32, (group, group), 0) < lax.broadcasted_iota(
        I32, (group, group), 1
    )
    rank = jnp.dot(
        jnp.where(wanted, 1.0, 0.0).astype(BF16),
        jnp.where(earlier, 1.0, 0.0).astype(BF16),
        preferred_element_type=F32,
    )
    place = jnp.where(wanted, rank, -1.0).astype(BF16)
    rows = replicas * CAP
    row = lax.broadcasted_iota(I32, (rows, replicas), 0)
    widen = (row // CAP) == lax.broadcasted_iota(I32, (rows, replicas), 1)
    place = jnp.dot(jnp.where(widen, 1.0, 0.0).astype(BF16), place, preferred_element_type=F32)
    own = (lax.broadcasted_iota(I32, (rows, group), 0) % CAP).astype(F32)
    hits = jnp.where(place == own, 1.0, 0.0).astype(BF16)
    sent = jnp.dot(hits, tokens_ref[...], preferred_element_type=F32).astype(BF16)
    out_ref[...] = sent.reshape(out_ref.shape)


def pack_kernel(gate_ref, up_ref, down_ref, out_ref):
    replicas = out_ref.shape[0]
    half = replicas // 2
    third = out_ref.shape[2] // 3
    for part, ref in enumerate((gate_ref, up_ref)):
        for side in range(2):
            block = ref[:, side * third : (side + 1) * third]
            out_ref[side * half : (side + 1) * half, :, part * third : (part + 1) * third] = (
                block.reshape(half, CAP, third)
            )
    fours = replicas // 4
    for side in range(4):
        block = down_ref[:, side * LANES : (side + 1) * LANES].reshape(fours, 3, CAP, LANES)
        for k in range(3):
            start = 2 * third + k * LANES
            out_ref[side * fours : (side + 1) * fours, :, start : start + LANES] = block[:, k]


def expand_kernel(place_ref, arrived_ref, gate_ref, up_ref, kept_ref, sent_ref):
    core = place_ref[1]
    chips, rows = kept_ref.shape[:2]
    hidden = gate_ref.shape[1]
    for ref, mine in ((sent_ref, 1 - core), (kept_ref, core)):
        for chip in range(chips):
            start = pl.multiple_of((2 * chip + mine) * rows, rows)
            block = arrived_ref[pl.ds(start, rows), :]
            for part, weight_ref in enumerate((gate_ref, up_ref)):
                ref[chip, :, part * hidden : (part + 1) * hidden] = jnp.dot(
                    block, weight_ref[...], preferred_element_type=F32
                ).astype(BF16)


def middle_kernel(place_ref, map_ref, spread_ref, own_ref, other_ref, down_ref, out_ref):
    chip, core = place_ref[0], place_ref[1]
    replicas, _, width = spread_ref.shape
    chips, rows = own_ref.shape[:2]
    groups = rows // CAP

    def move(old, carry):
        out_ref[map_ref[old], :, 0:width] = spread_ref[old]
        return carry

    lax.fori_loop(0, replicas, move, 0, unroll=8)
    for ref, mine in ((own_ref, core), (other_ref, 1 - core)):
        for step in range(chips):
            chunk = 2 * lax.rem(chip + step, chips) + mine
            made = jnp.dot(ref[step], down_ref[...], preferred_element_type=F32).astype(BF16)
            start = pl.multiple_of(chunk * groups, groups)
            out_ref[pl.ds(start, groups), :, width:] = made.reshape(groups, CAP, -1)


def final_kernel(
    ids_ref, keep_ref, gates_ref, map_ref, tokens_ref, landed_ref, mixed_ref, gate_ref, up_ref, down_ref
):
    replicas = map_ref.shape[1]
    group, share = tokens_ref.shape
    half, fours = replicas // 2, replicas // 4
    width = landed_ref.shape[2] - share
    third = width // 3
    for part, ref in enumerate((gate_ref, up_ref)):
        for side in range(2):
            block = landed_ref[
                side * half : (side + 1) * half, :, part * third : (part + 1) * third
            ]
            ref[:, side * third : (side + 1) * third] = block.reshape(half * CAP, third)
    for side in range(4):
        blocks = [
            landed_ref[
                side * fours : (side + 1) * fours,
                :,
                2 * third + k * LANES : 2 * third + (k + 1) * LANES,
            ].reshape(fours, 1, CAP, LANES)
            for k in range(3)
        ]
        down_ref[:, side * LANES : (side + 1) * LANES] = jnp.concatenate(blocks, axis=1).reshape(
            fours * 3 * CAP, LANES
        )

    ids = jnp.where(keep_ref[...] > 0, ids_ref[...], -1).T
    gates = gates_ref[...].T
    slot_of = map_ref[...]
    hits = [ids[:, k : k + 1] == slot_of for k in range(ids.shape[1])]
    wanted, weight = hits[0], jnp.where(hits[0], gates[:, 0:1], 0.0)
    for k in range(1, ids.shape[1]):
        wanted = wanted | hits[k]
        weight = weight + jnp.where(hits[k], gates[:, k : k + 1], 0.0)
    earlier = lax.broadcasted_iota(I32, (group, group), 1) < lax.broadcasted_iota(
        I32, (group, group), 0
    )
    rank = jnp.dot(
        jnp.where(earlier, 1.0, 0.0).astype(BF16),
        jnp.where(wanted, 1.0, 0.0).astype(BF16),
        preferred_element_type=F32,
    )
    place = jnp.where(wanted, rank, -1.0).astype(BF16)
    rows = replicas * CAP
    widen = lax.broadcasted_iota(I32, (replicas, rows), 0) == (
        lax.broadcasted_iota(I32, (replicas, rows), 1) // CAP
    )
    widen = jnp.where(widen, 1.0, 0.0).astype(BF16)
    place = jnp.dot(place, widen, preferred_element_type=F32)
    match = place == (lax.broadcasted_iota(I32, (group, rows), 1) % CAP).astype(F32)
    returned = landed_ref[:, :, width:].reshape(rows, share)
    total = tokens_ref[...].astype(F32)
    left = weight
    for _ in range(3):
        top = left.astype(BF16)
        left = left - top.astype(F32)
        spread = jnp.dot(top, widen, preferred_element_type=F32)
        factor = jnp.where(match, spread, 0.0).astype(BF16)
        total = total + jnp.dot(factor, returned, preferred_element_type=F32)
    mixed_ref[...] = total.astype(BF16)


def exchange(parts):
    return lax.all_to_all(parts, "expert", split_axis=0, concat_axis=0, tiled=True)


def hop(value, to):
    places = [(d, to(d // 2, d % 2)) for d in range(lax.axis_size("dp"))]
    return lax.ppermute(value, "dp", [(d, 2 * chip + core) for d, (chip, core) in places])


def pick(values, index):
    return lax.dynamic_index_in_dim(values, index, axis=0, keepdims=False)


def shards(tokens, route_ids, route_gates, keep_mask, old_gate, old_up, old_down, placement_map):
    replicas = lax.axis_size("expert")
    chips = lax.axis_size("dp") // 2
    share = tokens.shape[1]
    hidden_size = old_gate.shape[2]
    gate_local, up_local, down_local = old_gate[0], old_up[0], old_down[0]
    position = lax.axis_index("dp")
    chip, core = position // 2, position % 2
    place = jnp.stack([chip, core]).astype(I32)
    map_row = placement_map.reshape(1, replicas)
    width = 3 * share * hidden_size // (replicas * CAP)
    rows = replicas * CAP

    outgoing = call(
        dispatch_kernel,
        jax.ShapeDtypeStruct((replicas, CAP, share), BF16),
        [VMEM] * 4,
    )(route_ids.T, keep_mask.T, map_row, tokens)
    received = exchange(outgoing)

    pieces = call(
        pack_kernel, jax.ShapeDtypeStruct((replicas, CAP, width), BF16), [VMEM] * 3
    )(gate_local, up_local, down_local)
    pieces, received = lax.optimization_barrier((pieces, received))
    spread = exchange(pieces)

    piece_rows = rows // (2 * chips)
    part = jax.ShapeDtypeStruct((chips, piece_rows, 2 * hidden_size), BF16)
    kept, sent = call(
        expand_kernel,
        (part, part),
        [SMEM, VMEM, VMEM, VMEM],
        flops=4 * rows * share * hidden_size,
        moved=8 << 20,
    )(place, received.reshape(rows, share), gate_local, up_local)

    flip = lambda c: c ^ 1
    mirror = lambda c: chips - 1 - c
    pair = kept.astype(F32) + hop(sent, lambda c, k: (c, 1 - k)).astype(F32)
    pair = pair.astype(BF16)
    gates, ups = pair[:, :, :hidden_size], pair[:, :, hidden_size:]
    beside, across = flip(chip), mirror(chip)
    diagonal = flip(across)
    gate_sent = jnp.stack([pick(gates, beside), pick(gates, diagonal)])
    up_sent = jnp.stack([pick(ups, across), pick(ups, diagonal)])
    gate_got = hop(gate_sent, lambda c, k: (flip(c), k)).astype(F32)
    up_got = hop(up_sent, lambda c, k: (mirror(c), k)).astype(F32)
    gate_second = (pick(gates, across).astype(F32) + gate_got[1]).astype(BF16)
    up_second = (pick(ups, beside).astype(F32) + up_got[1]).astype(BF16)
    gate_last = hop(gate_second, lambda c, k: (mirror(c), k)).astype(F32)
    up_last = hop(up_second, lambda c, k: (flip(c), k)).astype(F32)
    gate_sum = pick(gates, chip).astype(F32) + gate_got[0] + gate_last
    up_sum = pick(ups, chip).astype(F32) + up_got[0] + up_last
    hidden = (jax.nn.silu(gate_sum) * up_sum).astype(BF16)
    own = jnp.stack(
        [hidden]
        + [hop(hidden, lambda c, k, s=s: ((c - s) % chips, k)) for s in range(1, chips)]
    )
    other = hop(own, lambda c, k: (c, 1 - k))

    joined = call(
        middle_kernel,
        jax.ShapeDtypeStruct((replicas, CAP, width + share), BF16),
        [SMEM, SMEM, VMEM, VMEM, VMEM, VMEM],
    )(place, placement_map, spread, own, other, down_local)
    landed = exchange(joined)

    mixed, new_gate, new_up, new_down = call(
        final_kernel,
        tuple(
            jax.ShapeDtypeStruct(a.shape, BF16) for a in (tokens, gate_local, up_local, down_local)
        ),
        [VMEM] * 6,
    )(route_ids.T, keep_mask.T, route_gates.T, map_row, tokens, landed)
    return (mixed, new_gate[None], new_up[None], new_down[None])


def solution(mesh):
    in_specs = (
        P("expert", "dp"),
        P("expert", None),
        P("expert", None),
        P("expert", None),
        P("expert", "dp", None),
        P("expert", "dp", None),
        P("expert", None, "dp"),
        P(),
    )
    out_specs = (
        P("expert", "dp"),
        P("expert", "dp", None),
        P("expert", "dp", None),
        P("expert", None, "dp"),
    )
    return jax.shard_map(shards, mesh=mesh, in_specs=in_specs, out_specs=out_specs, check_vma=False)
```

```python
import jax
import jax.numpy as jnp
from jax import lax
from jax.experimental import pallas as pl
from jax.experimental.pallas import tpu as pltpu
from jax.sharding import PartitionSpec as P

CAP = 16
LANES = 128
VMEM = pl.BlockSpec(memory_space=pltpu.VMEM)
SMEM = pl.BlockSpec(memory_space=pltpu.SMEM)
ANY = pl.BlockSpec(memory_space=pl.ANY)
F32, BF16, I32 = jnp.float32, jnp.bfloat16, jnp.int32


def call(kernel, out_shape, in_specs, limit=60, **more):
    many = isinstance(out_shape, (tuple, list))
    more.setdefault("out_specs", [VMEM] * len(out_shape) if many else VMEM)
    return pl.pallas_call(
        kernel,
        out_shape=out_shape,
        in_specs=in_specs,
        compiler_params=pltpu.CompilerParams(vmem_limit_bytes=limit * 1024 * 1024),
        **more,
    )


def dispatch_kernel(ids_ref, keep_ref, map_ref, tokens_ref, out_ref):
    replicas = map_ref.shape[1]
    group = tokens_ref.shape[0]
    ids = jnp.where(keep_ref[...] > 0, ids_ref[...], -1)
    same = lax.broadcasted_iota(I32, (replicas, replicas), 0) == lax.broadcasted_iota(
        I32, (replicas, replicas), 1
    )
    slot_of = jnp.sum(jnp.where(same, map_ref[...], 0), axis=1, keepdims=True)
    wanted = ids[0:1, :] == slot_of
    for k in range(1, ids.shape[0]):
        wanted = wanted | (ids[k : k + 1, :] == slot_of)
    earlier = lax.broadcasted_iota(I32, (group, group), 0) < lax.broadcasted_iota(
        I32, (group, group), 1
    )
    rank = jnp.dot(
        jnp.where(wanted, 1.0, 0.0).astype(BF16),
        jnp.where(earlier, 1.0, 0.0).astype(BF16),
        preferred_element_type=F32,
    )
    place = jnp.where(wanted, rank, -1.0).astype(BF16)
    rows = replicas * CAP
    row = lax.broadcasted_iota(I32, (rows, replicas), 0)
    widen = (row // CAP) == lax.broadcasted_iota(I32, (rows, replicas), 1)
    place = jnp.dot(jnp.where(widen, 1.0, 0.0).astype(BF16), place, preferred_element_type=F32)
    own = (lax.broadcasted_iota(I32, (rows, group), 0) % CAP).astype(F32)
    hits = jnp.where(place == own, 1.0, 0.0).astype(BF16)
    sent = jnp.dot(hits, tokens_ref[...], preferred_element_type=F32).astype(BF16)
    out_ref[...] = sent.reshape(out_ref.shape)


def pack_kernel(gate_ref, up_ref, down_ref, out_ref):
    replicas = out_ref.shape[0]
    half = replicas // 2
    third = out_ref.shape[2] // 3
    for part, ref in enumerate((gate_ref, up_ref)):
        for side in range(2):
            block = ref[:, side * third : (side + 1) * third]
            out_ref[side * half : (side + 1) * half, :, part * third : (part + 1) * third] = (
                block.reshape(half, CAP, third)
            )
    fours = replicas // 4
    for side in range(4):
        block = down_ref[:, side * LANES : (side + 1) * LANES].reshape(fours, 3, CAP, LANES)
        for k in range(3):
            start = 2 * third + k * LANES
            out_ref[side * fours : (side + 1) * fours, :, start : start + LANES] = block[:, k]


def expand_kernel(place_ref, arrived_ref, gate_ref, up_ref, out_ref):
    chips, rows = out_ref.shape[:2]
    hidden = gate_ref.shape[1]
    for chip in range(chips):
        start = pl.multiple_of((2 * chip + place_ref[0]) * rows, rows)
        block = arrived_ref[pl.ds(start, rows), :]
        for part, weight_ref in enumerate((gate_ref, up_ref)):
            out_ref[chip, :, part * hidden : (part + 1) * hidden] = jnp.dot(
                block, weight_ref[...], preferred_element_type=F32
            ).astype(BF16)


def produce_kernel(
    place_ref, own_ref, other_ref, down_ref, ids_ref, keep_ref, gates_ref, map_ref, made_ref, factor_ref
):
    chip, core = place_ref[0], place_ref[1]
    chips, rows = own_ref.shape[:2]
    groups = rows // CAP
    for ref, mine in ((own_ref, core), (other_ref, 1 - core)):
        for step in range(chips):
            chunk = 2 * lax.rem(chip + step, chips) + mine
            made = jnp.dot(ref[step], down_ref[...], preferred_element_type=F32).astype(BF16)
            start = pl.multiple_of(chunk * groups, groups)
            made_ref[pl.ds(start, groups)] = made.reshape(groups, CAP, -1)

    replicas = map_ref.shape[1]
    group = ids_ref.shape[1]
    ids = jnp.where(keep_ref[...] > 0, ids_ref[...], -1).T
    gates = gates_ref[...].T
    slot_of = map_ref[...]
    hits = [ids[:, k : k + 1] == slot_of for k in range(ids.shape[1])]
    wanted, weight = hits[0], jnp.where(hits[0], gates[:, 0:1], 0.0)
    for k in range(1, ids.shape[1]):
        wanted = wanted | hits[k]
        weight = weight + jnp.where(hits[k], gates[:, k : k + 1], 0.0)
    earlier = lax.broadcasted_iota(I32, (group, group), 1) < lax.broadcasted_iota(
        I32, (group, group), 0
    )
    rank = jnp.dot(
        jnp.where(earlier, 1.0, 0.0).astype(BF16),
        jnp.where(wanted, 1.0, 0.0).astype(BF16),
        preferred_element_type=F32,
    )
    place = jnp.where(wanted, rank, -1.0).astype(BF16)
    width = replicas * CAP
    widen = lax.broadcasted_iota(I32, (replicas, width), 0) == (
        lax.broadcasted_iota(I32, (replicas, width), 1) // CAP
    )
    widen = jnp.where(widen, 1.0, 0.0).astype(BF16)
    place = jnp.dot(place, widen, preferred_element_type=F32)
    match = place == (lax.broadcasted_iota(I32, (group, width), 1) % CAP).astype(F32)
    left = weight
    for term in range(factor_ref.shape[0]):
        top = left.astype(BF16)
        left = left - top.astype(F32)
        spread = jnp.dot(top, widen, preferred_element_type=F32)
        factor_ref[term] = jnp.where(match, spread, 0.0).astype(BF16)


def join_kernel(map_ref, spread_ref, made_ref, out_ref, sems):
    replicas, _, width = spread_ref.shape
    beside = pltpu.make_async_copy(
        made_ref, out_ref.at[:, :, pl.ds(width, made_ref.shape[2])], sems.at[0]
    )
    beside.start()

    def move(old, carry):
        pltpu.make_async_copy(
            spread_ref.at[old], out_ref.at[map_ref[old], :, pl.ds(0, width)], sems.at[1]
        ).start()
        return carry

    lax.fori_loop(0, replicas, move, 0, unroll=8)
    beside.wait()
    pltpu.make_async_copy(spread_ref, out_ref.at[:, :, pl.ds(0, width)], sems.at[1]).wait()


def final_kernel(factor_ref, tokens_ref, landed_ref, mixed_ref, gate_ref, up_ref, down_ref, total):
    step = pl.program_id(0)
    pieces = landed_ref.shape[0]
    share = tokens_ref.shape[1]
    width = landed_ref.shape[2] - share
    third = width // 3
    for part, ref in enumerate((gate_ref, up_ref)):
        ref[...] = landed_ref[:, :, part * third : (part + 1) * third].reshape(ref.shape)
    blocks = [
        landed_ref[:, :, 2 * third + k * LANES : 2 * third + (k + 1) * LANES].reshape(
            pieces, 1, CAP, LANES
        )
        for k in range(3)
    ]
    down_ref[...] = jnp.concatenate(blocks, axis=1).reshape(down_ref.shape)

    @pl.when(step == 0)
    def _():
        total[...] = tokens_ref[...].astype(F32)

    returned = landed_ref[:, :, width:].reshape(pieces * CAP, share)
    part = jnp.dot(factor_ref[0], returned, preferred_element_type=F32)
    for term in range(1, factor_ref.shape[0]):
        part = part + jnp.dot(factor_ref[term], returned, preferred_element_type=F32)
    total[...] += part

    @pl.when(step == pl.num_programs(0) - 1)
    def _():
        mixed_ref[...] = total[...].astype(BF16)


def exchange(parts):
    return lax.all_to_all(parts, "expert", split_axis=0, concat_axis=0, tiled=True)


def hop(value, to):
    places = [(d, to(d // 2, d % 2)) for d in range(lax.axis_size("dp"))]
    return lax.ppermute(value, "dp", [(d, 2 * chip + core) for d, (chip, core) in places])


def pick(values, index):
    return lax.dynamic_index_in_dim(values, index, axis=0, keepdims=False)


def shards(tokens, route_ids, route_gates, keep_mask, old_gate, old_up, old_down, placement_map):
    replicas = lax.axis_size("expert")
    chips = lax.axis_size("dp") // 2
    share = tokens.shape[1]
    hidden_size = old_gate.shape[2]
    gate_local, up_local, down_local = old_gate[0], old_up[0], old_down[0]
    position = lax.axis_index("dp")
    chip, core = position // 2, position % 2
    place = jnp.stack([chip, core]).astype(I32)
    map_row = placement_map.reshape(1, replicas)
    width = 3 * share * hidden_size // (replicas * CAP)
    rows = replicas * CAP

    outgoing = call(
        dispatch_kernel,
        jax.ShapeDtypeStruct((replicas, CAP, share), BF16),
        [VMEM] * 4,
    )(route_ids.T, keep_mask.T, map_row, tokens)
    received = exchange(outgoing)

    pieces = call(
        pack_kernel, jax.ShapeDtypeStruct((replicas, CAP, width), BF16), [VMEM] * 3
    )(gate_local, up_local, down_local)
    pieces, received = lax.optimization_barrier((pieces, received))
    spread = exchange(pieces)

    piece_rows = rows // (2 * chips)
    part = jax.ShapeDtypeStruct((chips, piece_rows, 2 * hidden_size), BF16)
    expand = call(expand_kernel, part, [SMEM, VMEM, VMEM, VMEM], limit=20)
    arrived = received.reshape(rows, share)
    sent = expand((1 - core).reshape(1).astype(I32), arrived, gate_local, up_local)
    kept = expand(core.reshape(1).astype(I32), arrived, gate_local, up_local)

    flip = lambda c: c ^ 1
    mirror = lambda c: chips - 1 - c
    pair = kept.astype(F32) + hop(sent, lambda c, k: (c, 1 - k)).astype(F32)
    pair = pair.astype(BF16)
    gates, ups = pair[:, :, :hidden_size], pair[:, :, hidden_size:]
    beside, across = flip(chip), mirror(chip)
    diagonal = flip(across)
    gate_sent = jnp.stack([pick(gates, beside), pick(gates, diagonal)])
    up_sent = jnp.stack([pick(ups, across), pick(ups, diagonal)])
    gate_got = hop(gate_sent, lambda c, k: (flip(c), k)).astype(F32)
    up_got = hop(up_sent, lambda c, k: (mirror(c), k)).astype(F32)
    gate_second = (pick(gates, across).astype(F32) + gate_got[1]).astype(BF16)
    up_second = (pick(ups, beside).astype(F32) + up_got[1]).astype(BF16)
    gate_last = hop(gate_second, lambda c, k: (mirror(c), k)).astype(F32)
    up_last = hop(up_second, lambda c, k: (flip(c), k)).astype(F32)
    gate_sum = pick(gates, chip).astype(F32) + gate_got[0] + gate_last
    up_sum = pick(ups, chip).astype(F32) + up_got[0] + up_last
    hidden = (jax.nn.silu(gate_sum) * up_sum).astype(BF16)
    own = jnp.stack(
        [hidden]
        + [hop(hidden, lambda c, k, s=s: ((c - s) % chips, k)) for s in range(1, chips)]
    )
    other = hop(own, lambda c, k: (c, 1 - k))

    routing = (route_ids.T, keep_mask.T, route_gates.T, map_row)
    made, factors = call(
        produce_kernel,
        (
            jax.ShapeDtypeStruct((replicas, CAP, share), BF16),
            jax.ShapeDtypeStruct((3, tokens.shape[0], rows), BF16),
        ),
        [SMEM] + [VMEM] * 7,
        limit=20,
    )(place, own, other, down_local, *routing)
    joined = call(
        join_kernel,
        jax.ShapeDtypeStruct((replicas, CAP, width + share), BF16),
        [SMEM, ANY, ANY],
        limit=8,
        out_specs=ANY,
        scratch_shapes=[pltpu.SemaphoreType.DMA((2,))],
    )(placement_map, spread, made)
    landed = exchange(joined)

    steps = 4
    group = tokens.shape[0]
    half = (share // 2, hidden_size // 2)
    mixed, new_gate, new_up, new_down = call(
        final_kernel,
        tuple(
            jax.ShapeDtypeStruct(a.shape, BF16) for a in (tokens, gate_local, up_local, down_local)
        ),
        [
            pl.BlockSpec((3, group, rows // steps), lambda j: (0, 0, j)),
            pl.BlockSpec((group, share), lambda j: (0, 0)),
            pl.BlockSpec((replicas // steps, CAP, width + share), lambda j: (j, 0, 0)),
        ],
        limit=16,
        grid=(steps,),
        out_specs=[
            pl.BlockSpec((group, share), lambda j: (0, 0)),
            pl.BlockSpec(half, lambda j: (j % 2, j // 2)),
            pl.BlockSpec(half, lambda j: (j % 2, j // 2)),
            pl.BlockSpec((hidden_size, LANES), lambda j: (0, j)),
        ],
        scratch_shapes=[pltpu.VMEM((group, share), F32)],
    )(factors, tokens, landed)
    return (mixed, new_gate[None], new_up[None], new_down[None])


def solution(mesh):
    in_specs = (
        P("expert", "dp"),
        P("expert", None),
        P("expert", None),
        P("expert", None),
        P("expert", "dp", None),
        P("expert", "dp", None),
        P("expert", None, "dp"),
        P(),
    )
    out_specs = (
        P("expert", "dp"),
        P("expert", "dp", None),
        P("expert", "dp", None),
        P("expert", None, "dp"),
    )
    return jax.shard_map(shards, mesh=mesh, in_specs=in_specs, out_specs=out_specs, check_vma=False)
```

```python
import jax
import jax.numpy as jnp
from jax import lax
from jax.experimental import pallas as pl
from jax.experimental.pallas import tpu as pltpu
from jax.sharding import PartitionSpec as P

CAP = 16
LANES = 128
VMEM = pl.BlockSpec(memory_space=pltpu.VMEM)
SMEM = pl.BlockSpec(memory_space=pltpu.SMEM)
ANY = pl.BlockSpec(memory_space=pl.ANY)
HBM = pl.BlockSpec(memory_space=pltpu.HBM)
F32, BF16, I32 = jnp.float32, jnp.bfloat16, jnp.int32


def call(kernel, out_shape, in_specs, limit=60, **more):
    many = isinstance(out_shape, (tuple, list))
    more.setdefault("out_specs", [VMEM] * len(out_shape) if many else VMEM)
    return pl.pallas_call(
        kernel,
        out_shape=out_shape,
        in_specs=in_specs,
        compiler_params=pltpu.CompilerParams(vmem_limit_bytes=limit * 1024 * 1024),
        **more,
    )


def dispatch_kernel(ids_ref, keep_ref, map_ref, tokens_ref, out_ref):
    replicas = map_ref.shape[1]
    group = tokens_ref.shape[0]
    ids = jnp.where(keep_ref[...] > 0, ids_ref[...], -1)
    same = lax.broadcasted_iota(I32, (replicas, replicas), 0) == lax.broadcasted_iota(
        I32, (replicas, replicas), 1
    )
    slot_of = jnp.sum(jnp.where(same, map_ref[...], 0), axis=1, keepdims=True)
    wanted = ids[0:1, :] == slot_of
    for k in range(1, ids.shape[0]):
        wanted = wanted | (ids[k : k + 1, :] == slot_of)
    earlier = lax.broadcasted_iota(I32, (group, group), 0) < lax.broadcasted_iota(
        I32, (group, group), 1
    )
    rank = jnp.dot(
        jnp.where(wanted, 1.0, 0.0).astype(BF16),
        jnp.where(earlier, 1.0, 0.0).astype(BF16),
        preferred_element_type=F32,
    )
    place = jnp.where(wanted, rank, -1.0).astype(BF16)
    rows = replicas * CAP
    row = lax.broadcasted_iota(I32, (rows, replicas), 0)
    widen = (row // CAP) == lax.broadcasted_iota(I32, (rows, replicas), 1)
    place = jnp.dot(jnp.where(widen, 1.0, 0.0).astype(BF16), place, preferred_element_type=F32)
    own = (lax.broadcasted_iota(I32, (rows, group), 0) % CAP).astype(F32)
    hits = jnp.where(place == own, 1.0, 0.0).astype(BF16)
    sent = jnp.dot(hits, tokens_ref[...], preferred_element_type=F32).astype(BF16)
    out_ref[...] = sent.reshape(out_ref.shape)


def pack_kernel(gate_ref, up_ref, down_ref, out_ref):
    replicas = out_ref.shape[0]
    half = replicas // 2
    third = out_ref.shape[2] // 3
    for part, ref in enumerate((gate_ref, up_ref)):
        for side in range(2):
            block = ref[:, side * third : (side + 1) * third]
            out_ref[side * half : (side + 1) * half, :, part * third : (part + 1) * third] = (
                block.reshape(half, CAP, third)
            )
    fours = replicas // 4
    for side in range(4):
        block = down_ref[:, side * LANES : (side + 1) * LANES].reshape(fours, 3, CAP, LANES)
        for k in range(3):
            start = 2 * third + k * LANES
            out_ref[side * fours : (side + 1) * fours, :, start : start + LANES] = block[:, k]


def expand_kernel(place_ref, arrived_ref, gate_hbm, up_hbm, out_ref, weights, sems):
    chips, rows = out_ref.shape[:2]
    hidden = weights.shape[2]
    copies = [
        pltpu.make_async_copy(ref, weights.at[k], sems.at[k])
        for k, ref in enumerate((gate_hbm, up_hbm))
    ]
    for copy in copies:
        copy.start()
    for part, copy in enumerate(copies):
        copy.wait()
        for chip in range(chips):
            start = pl.multiple_of((2 * chip + place_ref[0]) * rows, rows)
            out_ref[chip, :, part * hidden : (part + 1) * hidden] = jnp.dot(
                arrived_ref[pl.ds(start, rows), :], weights[part], preferred_element_type=F32
            ).astype(BF16)


def produce_kernel(
    place_ref, own_ref, other_ref, down_ref, ids_ref, keep_ref, gates_ref, map_ref, made_ref, factor_ref
):
    chip, core = place_ref[0], place_ref[1]
    chips, rows = own_ref.shape[:2]
    groups = rows // CAP
    for ref, mine in ((own_ref, core), (other_ref, 1 - core)):
        for step in range(chips):
            chunk = 2 * lax.rem(chip + step, chips) + mine
            made = jnp.dot(ref[step], down_ref[...], preferred_element_type=F32).astype(BF16)
            start = pl.multiple_of(chunk * groups, groups)
            made_ref[pl.ds(start, groups)] = made.reshape(groups, CAP, -1)

    replicas = map_ref.shape[1]
    group = ids_ref.shape[1]
    ids = jnp.where(keep_ref[...] > 0, ids_ref[...], -1).T
    gates = gates_ref[...].T
    slot_of = map_ref[...]
    hits = [ids[:, k : k + 1] == slot_of for k in range(ids.shape[1])]
    wanted, weight = hits[0], jnp.where(hits[0], gates[:, 0:1], 0.0)
    for k in range(1, ids.shape[1]):
        wanted = wanted | hits[k]
        weight = weight + jnp.where(hits[k], gates[:, k : k + 1], 0.0)
    earlier = lax.broadcasted_iota(I32, (group, group), 1) < lax.broadcasted_iota(
        I32, (group, group), 0
    )
    rank = jnp.dot(
        jnp.where(earlier, 1.0, 0.0).astype(BF16),
        jnp.where(wanted, 1.0, 0.0).astype(BF16),
        preferred_element_type=F32,
    )
    place = jnp.where(wanted, rank, -1.0).astype(BF16)
    width = replicas * CAP
    widen = lax.broadcasted_iota(I32, (replicas, width), 0) == (
        lax.broadcasted_iota(I32, (replicas, width), 1) // CAP
    )
    widen = jnp.where(widen, 1.0, 0.0).astype(BF16)
    place = jnp.dot(place, widen, preferred_element_type=F32)
    match = place == (lax.broadcasted_iota(I32, (group, width), 1) % CAP).astype(F32)
    left = weight
    for term in range(factor_ref.shape[0]):
        top = left.astype(BF16)
        left = left - top.astype(F32)
        spread = jnp.dot(top, widen, preferred_element_type=F32)
        factor_ref[term] = jnp.where(match, spread, 0.0).astype(BF16)


def join_kernel(map_ref, spread_ref, made_ref, out_ref, sems):
    replicas, _, width = spread_ref.shape
    beside = pltpu.make_async_copy(
        made_ref, out_ref.at[:, :, pl.ds(width, made_ref.shape[2])], sems.at[0]
    )
    beside.start()

    def move(old, carry):
        pltpu.make_async_copy(
            spread_ref.at[old], out_ref.at[map_ref[old], :, pl.ds(0, width)], sems.at[1]
        ).start()
        return carry

    lax.fori_loop(0, replicas, move, 0, unroll=8)
    beside.wait()
    pltpu.make_async_copy(spread_ref, out_ref.at[:, :, pl.ds(0, width)], sems.at[1]).wait()


def final_kernel(factor_ref, tokens_ref, landed_ref, mixed_ref, gate_ref, up_ref, down_ref, total):
    step = pl.program_id(0)
    pieces = landed_ref.shape[0]
    share = tokens_ref.shape[1]
    width = landed_ref.shape[2] - share
    third = width // 3
    for part, ref in enumerate((gate_ref, up_ref)):
        ref[...] = landed_ref[:, :, part * third : (part + 1) * third].reshape(ref.shape)
    blocks = [
        landed_ref[:, :, 2 * third + k * LANES : 2 * third + (k + 1) * LANES].reshape(
            pieces, 1, CAP, LANES
        )
        for k in range(3)
    ]
    down_ref[...] = jnp.concatenate(blocks, axis=1).reshape(down_ref.shape)

    @pl.when(step == 0)
    def _():
        total[...] = tokens_ref[...].astype(F32)

    returned = landed_ref[:, :, width:].reshape(pieces * CAP, share)
    part = jnp.dot(factor_ref[0], returned, preferred_element_type=F32)
    for term in range(1, factor_ref.shape[0]):
        part = part + jnp.dot(factor_ref[term], returned, preferred_element_type=F32)
    total[...] += part

    @pl.when(step == pl.num_programs(0) - 1)
    def _():
        mixed_ref[...] = total[...].astype(BF16)


def exchange(parts):
    return lax.all_to_all(parts, "expert", split_axis=0, concat_axis=0, tiled=True)


def hop(value, to):
    places = [(d, to(d // 2, d % 2)) for d in range(lax.axis_size("dp"))]
    return lax.ppermute(value, "dp", [(d, 2 * chip + core) for d, (chip, core) in places])


def pick(values, index):
    return lax.dynamic_index_in_dim(values, index, axis=0, keepdims=False)


def shards(tokens, route_ids, route_gates, keep_mask, old_gate, old_up, old_down, placement_map):
    replicas = lax.axis_size("expert")
    chips = lax.axis_size("dp") // 2
    share = tokens.shape[1]
    hidden_size = old_gate.shape[2]
    gate_local, up_local, down_local = old_gate[0], old_up[0], old_down[0]
    position = lax.axis_index("dp")
    chip, core = position // 2, position % 2
    place = jnp.stack([chip, core]).astype(I32)
    map_row = placement_map.reshape(1, replicas)
    width = 3 * share * hidden_size // (replicas * CAP)
    rows = replicas * CAP

    outgoing = call(
        dispatch_kernel,
        jax.ShapeDtypeStruct((replicas, CAP, share), BF16),
        [VMEM] * 4,
    )(route_ids.T, keep_mask.T, map_row, tokens)
    received = exchange(outgoing)

    pieces = call(
        pack_kernel, jax.ShapeDtypeStruct((replicas, CAP, width), BF16), [VMEM] * 3
    )(gate_local, up_local, down_local)
    pieces, received = lax.optimization_barrier((pieces, received))
    spread = exchange(pieces)

    piece_rows = rows // (2 * chips)
    part = jax.ShapeDtypeStruct((chips, piece_rows, 2 * hidden_size), BF16)
    def expand(first, flops):
        return call(
            expand_kernel,
            part,
            [SMEM, VMEM, HBM, HBM],
            limit=20,
            scratch_shapes=[
                pltpu.VMEM((2,) + gate_local.shape, BF16),
                pltpu.SemaphoreType.DMA((2,)),
            ],
            cost_estimate=pl.CostEstimate(flops=flops, bytes_accessed=0, transcendentals=0),
        )(first.reshape(1).astype(I32), arrived, gate_local, up_local)

    arrived = received.reshape(rows, share)
    flops = 2 * rows * share * hidden_size
    sent = expand(1 - core, flops)
    kept = expand(core, 64 * flops)

    flip = lambda c: c ^ 1
    mirror = lambda c: chips - 1 - c
    pair = kept.astype(F32) + hop(sent, lambda c, k: (c, 1 - k)).astype(F32)
    pair = pair.astype(BF16)
    gates, ups = pair[:, :, :hidden_size], pair[:, :, hidden_size:]
    beside, across = flip(chip), mirror(chip)
    diagonal = flip(across)
    gate_sent = jnp.stack([pick(gates, beside), pick(gates, diagonal)])
    up_sent = jnp.stack([pick(ups, across), pick(ups, diagonal)])
    gate_got = hop(gate_sent, lambda c, k: (flip(c), k)).astype(F32)
    up_got = hop(up_sent, lambda c, k: (mirror(c), k)).astype(F32)
    gate_second = (pick(gates, across).astype(F32) + gate_got[1]).astype(BF16)
    up_second = (pick(ups, beside).astype(F32) + up_got[1]).astype(BF16)
    gate_last = hop(gate_second, lambda c, k: (mirror(c), k)).astype(F32)
    up_last = hop(up_second, lambda c, k: (flip(c), k)).astype(F32)
    gate_sum = pick(gates, chip).astype(F32) + gate_got[0] + gate_last
    up_sum = pick(ups, chip).astype(F32) + up_got[0] + up_last
    hidden = (jax.nn.silu(gate_sum) * up_sum).astype(BF16)
    own = jnp.stack(
        [hidden]
        + [hop(hidden, lambda c, k, s=s: ((c - s) % chips, k)) for s in range(1, chips)]
    )
    other = hop(own, lambda c, k: (c, 1 - k))

    routing = (route_ids.T, keep_mask.T, route_gates.T, map_row)
    made, factors = call(
        produce_kernel,
        (
            jax.ShapeDtypeStruct((replicas, CAP, share), BF16),
            jax.ShapeDtypeStruct((3, tokens.shape[0], rows), BF16),
        ),
        [SMEM] + [VMEM] * 7,
        limit=20,
    )(place, own, other, down_local, *routing)
    joined = call(
        join_kernel,
        jax.ShapeDtypeStruct((replicas, CAP, width + share), BF16),
        [SMEM, ANY, ANY],
        limit=8,
        out_specs=ANY,
        scratch_shapes=[pltpu.SemaphoreType.DMA((2,))],
    )(placement_map, spread, made)
    landed = exchange(joined)

    steps = 4
    group = tokens.shape[0]
    half = (share // 2, hidden_size // 2)
    mixed, new_gate, new_up, new_down = call(
        final_kernel,
        tuple(
            jax.ShapeDtypeStruct(a.shape, BF16) for a in (tokens, gate_local, up_local, down_local)
        ),
        [
            pl.BlockSpec((3, group, rows // steps), lambda j: (0, 0, j)),
            pl.BlockSpec((group, share), lambda j: (0, 0)),
            pl.BlockSpec((replicas // steps, CAP, width + share), lambda j: (j, 0, 0)),
        ],
        limit=16,
        grid=(steps,),
        out_specs=[
            pl.BlockSpec((group, share), lambda j: (0, 0)),
            pl.BlockSpec(half, lambda j: (j % 2, j // 2)),
            pl.BlockSpec(half, lambda j: (j % 2, j // 2)),
            pl.BlockSpec((hidden_size, LANES), lambda j: (0, j)),
        ],
        scratch_shapes=[pltpu.VMEM((group, share), F32)],
    )(factors, tokens, landed)
    return (mixed, new_gate[None], new_up[None], new_down[None])


def solution(mesh):
    in_specs = (
        P("expert", "dp"),
        P("expert", None),
        P("expert", None),
        P("expert", None),
        P("expert", "dp", None),
        P("expert", "dp", None),
        P("expert", None, "dp"),
        P(),
    )
    out_specs = (
        P("expert", "dp"),
        P("expert", "dp", None),
        P("expert", "dp", None),
        P("expert", None, "dp"),
    )
    return jax.shard_map(shards, mesh=mesh, in_specs=in_specs, out_specs=out_specs, check_vma=False)
```
